512 devices in a mesh: dp: 8 (over z_lo), ctx: 64 (over z_hi, y, x, core).
Axes of the slice: x: 4, y: 4, z: 16 (z_hi: 2, z_lo: 8; z = z_hi * 8 + z_lo), core: 2. Of those that a mesh axis runs over, the one named last changes fastest.
Arguments:
- fwd_proj: bfloat16 [65536, 3072], P(('dp', 'ctx')), parts along dimension 0, may hold values from -6 to 6
- rev_proj: bfloat16 [65536, 3072], P(('dp', 'ctx')), parts along dimension 0, may hold values from -6 to 6
- tokens: int32 [65536], P(('dp', 'ctx')), parts along dimension 0, may hold values from 0 to 4
- short_taps: float32 [3, 3072], replicated, may hold values from -3.5 to 3.5
- long_kernel: float32 [1024, 8192], P('ctx'), may hold values from -1 to 1
- skip_gain: float32 [1024], P('ctx'), may hold values from -4 to 4
- out_weight: bfloat16 [1024, 1024], replicated, may hold values from -0.1875 to 0.1875
Outputs:
- mixed: bfloat16 [65536, 1024], P(('dp', 'ctx')), parts along dimension 0
The draws below stay inside these ranges and needn't reach their ends.
There are 8 independent parts, one for each index of `dp`. The reference program is written for one: setup_inputs(seed, part) draws one part's arguments, and reference() takes and returns one part's arrays. A program takes and returns all parts, laid end to end along the dimension named above; an argument that names none is the same for every part. Nothing has to cross between parts.
Inputs may be any that keep to these rules, and one draw needn't show every extreme that they name: `tokens`: base of each position, 0 to 3 for A, C, G, T and 4 for an unknown base N.
All inputs are finite; a program needn't handle non-finite values.
Results may differ from the reference program's by a relative error of at most 0.0064.
Values may be sent and summed in bfloat16 or wider, within the bound.
A program may use at most 64 MiB of HBM per device.

```python
import math
import jax
import jax.numpy as jnp

D = 1024
SEQ = 8192


def draw_long_kernel(key, part):
    key = jax.random.fold_in(key, 7)
    rate_key, base_key = jax.random.split(key)
    rates = jnp.exp(jax.random.uniform(rate_key, (D, 1), jnp.float32, math.log(0.5), math.log(8.0)))
    lags = jnp.arange(SEQ, dtype=jnp.float32)[None, :] / SEQ
    envelope = jnp.exp(-rates * lags)
    base = jnp.clip(jax.random.normal(base_key, (D, SEQ), jnp.float32), -4.0, 4.0)
    return 2.0 * base * envelope / math.sqrt(SEQ)


def with_ends(drawn, stream_key, least, largest):
    longest = drawn.shape.index(max(drawn.shape))
    spots = []
    for shift in (0, 1):
        where = [jax.random.randint(jax.random.fold_in(stream_key, axis), (), 0, length) for axis, length in enumerate(drawn.shape)]
        where[longest] = (where[longest] + shift) % drawn.shape[longest]
        spots.append(tuple(where))
    return drawn.at[spots[0]].set(least).at[spots[1]].set(largest)


def steps_of(rng, extent, pieces, low, high):
    level = 1.0
    for dim, shards_of in pieces:
        heights = jax.random.uniform(jax.random.fold_in(jax.random.fold_in(rng, 6), dim), (shards_of,), jnp.float32, low / len(pieces), high / len(pieces))
        level = level * jnp.repeat(jnp.exp(heights), extent[dim] // shards_of).reshape((-1,) + (1,) * (len(extent) - 1 - dim))
    return level


def bell_draw(own_key, shape, deviation, reach, cuts=(), kind=jnp.bfloat16):
    result = jax.random.normal(own_key, shape, jnp.float32) * deviation
    if len(cuts) > 0:
        result = steps_of(own_key, shape, cuts, -0.22, 0.18) * result
    return jnp.clip(result, min=-reach, max=reach).astype(kind)


def setup_inputs(seed: int = 0, part: int = 0) -> dict:
    key_of = jax.random.split(jax.random.key(seed), 8)
    part_splits = jax.random.split(jax.random.fold_in(key_of[7], part), 8)
    return {
        "fwd_proj": bell_draw(part_splits[0], (SEQ, 3 * D), 1.0, 6.0, ((0, 64),)),
        "rev_proj": bell_draw(part_splits[1], (SEQ, 3 * D), 1.0, 6.0, ((0, 64),)),
        "tokens": with_ends(jax.random.randint(part_splits[2], (SEQ,), 0, 5), jax.random.fold_in(part_splits[2], 1), 0, 4).astype(jnp.int32),
        "short_taps": bell_draw(key_of[3], (3, 3 * D), 3 ** -0.5, 3.5, (), jnp.float32),
        "long_kernel": draw_long_kernel(jax.random.fold_in(key_of[7], 71), part),
        "skip_gain": bell_draw(key_of[5], (D,), 1.0, 4.0, ((0, 64),), jnp.float32),
        "out_weight": bell_draw(key_of[6], (D, D), D ** -0.5, 0.1875),
    }


def long_filter(signal, spectrum, skip_gain):
    columns = signal.astype(jnp.float32).T
    product = jnp.fft.rfft(columns, n=2 * SEQ, axis=1) * spectrum
    filtered = jnp.fft.irfft(product, n=2 * SEQ, axis=1)[:, :SEQ]
    return (filtered + skip_gain[:, None] * columns).T.astype(jnp.bfloat16)


def reference(fwd_proj, rev_proj, tokens, short_taps, long_kernel, skip_gain, out_weight):
    fwd_rows = fwd_proj.astype(jnp.float32)
    rev_rows = rev_proj.astype(jnp.float32)
    blank = jnp.zeros((2, fwd_rows.shape[1]), jnp.float32)
    fwd_ext = jnp.concatenate([blank, fwd_rows], axis=0)
    rev_ext = jnp.concatenate([rev_rows, blank], axis=0)
    fwd_mixed = short_taps[0] * fwd_ext[2:] + short_taps[1] * fwd_ext[1:-1] + short_taps[2] * fwd_ext[:-2]
    rev_mixed = short_taps[0] * rev_ext[:-2] + short_taps[1] * rev_ext[1:-1] + short_taps[2] * rev_ext[2:]
    known = (tokens != 4).astype(jnp.float32)[:, None]
    fwd_input = (known * fwd_mixed[:, D:2 * D] * fwd_mixed[:, :D]).astype(jnp.bfloat16)
    rev_input = (known * rev_mixed[:, D:2 * D] * rev_mixed[:, :D]).astype(jnp.bfloat16)
    spectrum = jnp.fft.rfft(long_kernel, n=2 * SEQ, axis=1)
    fwd_out = long_filter(fwd_input, spectrum, skip_gain)
    rev_out = long_filter(rev_input[::-1], spectrum, skip_gain)[::-1]
    fwd_gated = fwd_mixed[:, 2 * D:] * fwd_out.astype(jnp.float32)
    rev_gated = rev_mixed[:, 2 * D:] * rev_out.astype(jnp.float32)
    combined = (fwd_gated + rev_gated[:, ::-1]).astype(jnp.bfloat16)
    return jnp.dot(combined, out_weight, preferred_element_type=jnp.float32).astype(jnp.bfloat16)
```

```python
import functools

import jax
import jax.numpy as jnp
from jax import lax
from jax.experimental import pallas as pl
from jax.experimental.pallas import tpu as pltpu
from jax.sharding import PartitionSpec as P

F32, BF16, I32 = jnp.float32, jnp.bfloat16, jnp.int32
MESH = pl.DeviceIdType.MESH
D = 1024
POS = 128
NB = 32
CH = 16
PAD = 16
SB = PAD + NB + 16
LINE = 8


def eye(flip):
    row = lax.broadcasted_iota(I32, (POS, POS), 0)
    col = lax.broadcasted_iota(I32, (POS, POS), 1)
    return (row == jnp.where(flip, POS - 1 - col, col)).astype(F32).astype(BF16)


def low_half(rows):
    return lax.broadcasted_iota(I32, (rows, 128), 1) < 64


def build_taps(rows_ref, first, out):
    row = lax.broadcasted_iota(I32, (8, 128), 0)
    lane = lax.broadcasted_iota(I32, (8, 128), 1)
    masks = [lane >= row + 8 * k for k in range(8)]

    def step(jb, before):
        rows = rows_ref[pl.ds(pl.multiple_of(first + jb * 16, 16), 16), :].astype(F32)
        for jj in range(16):
            wide = jnp.broadcast_to(rows[jj : jj + 1], (8, 128))
            now = [pltpu.roll(wide, 8 * k, 1, stride=1, stride_axis=0) for k in range(8)]
            for k in range(4):
                top = jnp.where(masks[2 * k], now[2 * k], before[2 * k])
                low = jnp.where(masks[2 * k + 1], now[2 * k + 1], before[2 * k + 1])
                at = pl.multiple_of((jb * 8 + jj // 2) * 64 + 16 * k, 16)
                out[pl.ds(at, 16), pl.ds(128 * (jj % 2), 128)] = jnp.concatenate(
                    [top, low], axis=0
                ).astype(BF16)
            before = now
        return tuple(before)

    lax.fori_loop(0, 4, step, (jnp.zeros((8, 128), F32),) * 8)


def halves(staged, c, start, rows):
    low = low_half(rows)
    for p in range(4):
        near = staged[pl.ds((PAD + start - 4 * p) * CH + c, rows, stride=CH), :]
        far = staged[pl.ds((PAD + start - 4 * p - 2) * CH + c, rows, stride=CH), :]
        even = jnp.where(low, near, pltpu.roll(far, 64, 1)).astype(BF16)
        odd = jnp.where(low, pltpu.roll(near, 64, 1), far).astype(BF16)
        yield p, even, odd


def overlap(parts, at):
    low = low_half(NB)

    def load(par, off, col):
        return parts[par, pl.ds(at + off, NB), pl.ds(col, 128)]

    mix = jnp.where(low, load(1, 0, 0), load(1, -1, 0)) + jnp.where(
        low, load(1, -1, 128), load(1, -2, 128)
    )
    return load(0, 0, 0) + load(0, -1, 128) + pltpu.roll(mix, 64, 1)


def near_filter(c, taps, sig_a, sig_b, out_a, out_b, lhs, part_a, part_b):
    for which, staged in enumerate((sig_a, sig_b)):
        base = 2 * NB * which
        for p, even, odd in halves(staged, c, 0, NB):
            for s in range(2):
                col = pl.ds(512 * s + 128 * p, 128)
                lhs[base + 16 * s : base + NB, col] = even[: NB - 16 * s]
                lhs[base + NB + 16 * s : base + 2 * NB, col] = odd[: NB - 16 * s]
    acc = jnp.dot(lhs[...], taps[: 4 * 256, :], preferred_element_type=F32)
    at = pl.ds(c, NB, stride=CH)
    for i, (part, out) in enumerate(((part_a, out_a), (part_b, out_b))):
        for par in range(2):
            part[par, 8 : 8 + NB, :] = acc[(2 * i + par) * NB : (2 * i + par + 1) * NB]
        out[at, :] = overlap(part, 8)


def far_filter(c, taps, sig, out, lhs, part):
    for p, even, odd in halves(sig, c, -2, 48):
        for s in range(4):
            col = pl.ds(512 * s + 128 * p, 128)
            src = 32 - 16 * s
            dst = max(0, -src)
            src = max(0, src)
            count = min(48 - src, 48 - dst)
            lhs[dst : dst + count, col] = even[src : src + count]
            lhs[48 + dst : 48 + dst + count, col] = odd[src : src + count]
    acc = jnp.dot(lhs[...], taps[...], preferred_element_type=F32)
    part[0, :, :] = acc[:48]
    part[1, :, :] = acc[48:]
    at = pl.ds(c, NB, stride=CH)
    out[at, :] = out[at, :] + overlap(part, 2)


def kernel(
    fwd, rev, tok, taps, lk, skip, weight, out,
    xin, xf, hsend, halo, z, hf, hk, g, ra, rb, rr, sa, sb, sr, ya, yb, ysa, ysb, yt,
    lhs_n, lhs_f, pa, pb, pf, o, wv, wr, cn, lkv,
    in_sem, halo_s, halo_r, up_s, up_r, dn_s, dn_r, z_s, z_r, y_s, y_r,
):
    dp = lax.axis_index("dp")
    ctx = lax.axis_index("ctx")
    h = ctx // NB
    r = ctx - h * NB
    slot = jnp.where(h == 0, r, NB - 1 - r)
    up = (lax.rem(dp + 1, LINE), jnp.where(dp == LINE - 1, 1 - h, h) * NB + r)
    down = (lax.rem(dp + LINE - 1, LINE), jnp.where(dp == 0, 1 - h, h) * NB + r)

    def plane(half, j):
        return half * NB + lax.rem(r + j, NB)

    @pl.when(h == 0)
    def _():
        pltpu.make_async_copy(fwd, xin.at[0], in_sem.at[0]).start()
        pltpu.make_async_copy(rev, xin.at[1], in_sem.at[1]).start()

    @pl.when(h == 1)
    def _():
        pltpu.make_async_copy(rev, xin.at[0], in_sem.at[0]).start()
        pltpu.make_async_copy(fwd, xin.at[1], in_sem.at[1]).start()

    pltpu.make_async_copy(lk, lkv, in_sem.at[2]).start()
    pltpu.make_async_copy(weight, wv, in_sem.at[3]).start()

    barrier = pltpu.get_barrier_semaphore()

    def greet(j, _):
        pl.semaphore_signal(barrier, inc=1, device_id=(dp, plane(1 - h, j)), device_id_type=MESH)

        @pl.when(j > 0)
        def _():
            pl.semaphore_signal(barrier, inc=1, device_id=(dp, plane(h, j)), device_id_type=MESH)

        return 0

    lax.fori_loop(0, NB, greet, 0)
    pl.semaphore_signal(barrier, inc=1, device_id=up, device_id_type=MESH)
    pl.semaphore_signal(barrier, inc=1, device_id=down, device_id_type=MESH)

    for ref in (sa, sb, sr, lhs_n, lhs_f, pa, pb):
        ref[...] = jnp.zeros_like(ref)

    pltpu.make_async_copy(lk, lkv, in_sem.at[2]).wait()
    first = lax.broadcasted_iota(I32, (CH, 128), 1) == 0
    for j in range(64):
        v = lkv[:, 128 * j : 128 * j + 128]
        if j == 0:
            v = v + jnp.where(first, skip[...], 0.0)
        hf[pl.ds(j, CH, stride=64), :] = v
    hk[0, :, :] = hf[...].astype(BF16)

    flips = (eye(h == 1), eye(h == 0))
    for role in range(2):
        pltpu.make_async_copy(fwd, xin.at[role], in_sem.at[role]).wait()
        for i in range(6):
            col = pl.ds(512 * i, 512)
            x = jnp.dot(flips[role], xin[role, :, col], preferred_element_type=F32)
            xf[role, 8 : 8 + POS, col] = x
            hsend[role, :, col] = x[POS - 16 :].astype(BF16)

    pl.semaphore_wait(barrier, 2 * NB - 1 + 2)

    def piece(buf, c):
        return hk.at[buf, pl.ds(pl.multiple_of(c * 64, 64), 64)]

    def up_copy(buf, i):
        return pltpu.make_async_remote_copy(
            src_ref=piece(buf, i), dst_ref=piece(1, i), send_sem=up_s.at[i],
            recv_sem=up_r.at[i], device_id=up, device_id_type=MESH,
        )

    def dn_copy(buf, i):
        return pltpu.make_async_remote_copy(
            src_ref=piece(buf, i + 8), dst_ref=piece(1, i + 8), send_sem=dn_s.at[i],
            recv_sem=dn_r.at[i], device_id=down, device_id_type=MESH,
        )

    at_end = slot == NB - 1
    inner = jnp.where(h == 0, r + 1, r - 1)
    turn = jnp.where(h == 0, 0, NB - 1)
    next_a = jnp.where(at_end, (1 - h) * NB + turn, h * NB + inner)
    next_b = h * NB + jnp.where(h == 0, r - 1, r + 1)

    def halo_copy(src, dst, to):
        return pltpu.make_async_remote_copy(
            src_ref=hsend.at[src], dst_ref=halo.at[dst], send_sem=halo_s.at[src],
            recv_sem=halo_r.at[dst], device_id=(dp, to), device_id_type=MESH,
        )

    @pl.when(at_end)
    def _():
        halo_copy(0, 1, next_a).start()

    @pl.when(jnp.logical_not(at_end))
    def _():
        halo_copy(0, 0, next_a).start()

    @pl.when(slot > 0)
    def _():
        halo_copy(1, 1, next_b).start()

    @pl.when(dp == LINE - 1)
    def _():
        def go(i, _):
            up_copy(0, i).start()
            return 0

        lax.fori_loop(0, 8, go, 0)

    @pl.when(dp == 0)
    def _():
        def go(i, _):
            dn_copy(0, i).start()
            return 0

        lax.fori_loop(0, 8, go, 0)

    known = (tok[...] != 4).astype(F32).astype(BF16)
    known = jnp.broadcast_to(known, (16, POS))

    def short(role, col):
        return (
            taps[0:1, col] * xf[role, 8 : 8 + POS, col]
            + taps[1:2, col] * xf[role, 7 : 7 + POS, col]
            + taps[2:3, col] * xf[role, 6 : 6 + POS, col]
        )

    def gate(role):
        mask = jnp.dot(known, flips[role], preferred_element_type=F32)[0:1]

        def tile(i, _):
            v = short(role, pl.ds(pl.multiple_of(128 * i, 128), 128))
            q = short(role, pl.ds(pl.multiple_of(128 * i + D, 128), 128))
            rows = pl.ds(pl.multiple_of(128 * i, 128), 128)
            z[role, rows, :] = (jnp.transpose(q * v) * mask).astype(BF16)
            return 0

        lax.fori_loop(0, D // 128, tile, 0)

    def z_rows(role, half, k, who):
        group = lax.rem(half + k, 2)
        return z.at[role, pl.ds(pl.multiple_of(group * (D // 2) + CH * who, CH), CH)]

    def send_near(role, k, buf, at):
        pltpu.make_async_copy(z_rows(role, h, k, r), buf.at[k, at], z_r.at[role, k]).start()

        def go(j, _):
            who = lax.rem(r + j, NB)
            pltpu.make_async_remote_copy(
                src_ref=z_rows(role, h, k, who), dst_ref=buf.at[k, at],
                send_sem=z_s.at[role, k], recv_sem=z_r.at[role, k],
                device_id=(dp, h * NB + who), device_id_type=MESH,
            ).start()
            return 0

        lax.fori_loop(1, NB, go, 0)

    def send_far(k):
        def go(j, _):
            who = lax.rem(r + j, NB)
            pltpu.make_async_remote_copy(
                src_ref=z_rows(0, 1 - h, k, who), dst_ref=rr.at[k, slot],
                send_sem=z_s.at[2, k], recv_sem=z_r.at[2, k],
                device_id=(dp, (1 - h) * NB + who), device_id_type=MESH,
            ).start()
            return 0

        lax.fori_loop(0, NB, go, 0)

    @pl.when(slot > 0)
    def _():
        pltpu.make_async_copy(halo.at[0], halo.at[0], halo_r.at[0]).wait()
        xf[0, 0:8, :] = halo[0, :, :].astype(F32)[8:16]

    @pl.when(slot == 0)
    def _():
        xf[0, 0:8, :] = jnp.zeros((8, 3 * D), F32)

    gate(0)
    send_far(0)
    send_near(0, 0, ra, slot)
    pltpu.make_async_copy(halo.at[1], halo.at[1], halo_r.at[1]).wait()
    xf[1, 0:8, :] = halo[1, :, :].astype(F32)[8:16]
    gate(1)
    send_near(1, 0, rb, NB - 1 - slot)
    send_far(1)
    send_near(0, 1, ra, slot)
    send_near(1, 1, rb, NB - 1 - slot)

    def own(i, _):
        iu = i - dp
        idn = i - (LINE - 1 - dp)

        @pl.when(jnp.logical_and(iu >= 0, iu < 8))
        def _():
            pltpu.make_async_copy(piece(1, iu), piece(1, iu), up_r.at[iu]).wait()

            @pl.when(dp < LINE - 1)
            def _():
                up_copy(1, iu).start()

        @pl.when(jnp.logical_and(idn >= 0, idn < 8))
        def _():
            pltpu.make_async_copy(piece(1, idn + 8), piece(1, idn + 8), dn_r.at[idn]).wait()

            @pl.when(dp > 0)
            def _():
                dn_copy(1, idn).start()

        build_taps(hk.at[0], i * 64, g.at[i])
        return 0

    lax.fori_loop(0, CH, own, 0)

    def stage(buf, sem, k, staged):
        pltpu.make_async_copy(buf.at[k], buf.at[k], sem).wait()
        staged[PAD * CH : (PAD + NB) * CH, :] = (
            buf[k, :, :, :].reshape(NB * CH, 128).astype(F32)
        )

    def give(role, k, src, send, base):
        send[k, :, :, :] = src[...].astype(BF16).reshape(NB, CH, 128)
        group = lax.rem(h + k, 2)
        rows = pl.ds(pl.multiple_of(group * (D // 2) + CH * r, CH), CH)

        def at(who):
            s = jnp.where(h == 0, who, NB - 1 - who)
            return s if role == 0 else NB - 1 - s

        pltpu.make_async_copy(send.at[k, at(r)], yt.at[role, rows], y_r.at[role, k]).start()

        def go(j, _):
            who = lax.rem(r + j, NB)
            pltpu.make_async_remote_copy(
                src_ref=send.at[k, at(who)], dst_ref=yt.at[role, rows],
                send_sem=y_s.at[role, k], recv_sem=y_r.at[role, k],
                device_id=(dp, h * NB + who), device_id_type=MESH,
            ).start()
            return 0

        lax.fori_loop(1, NB, go, 0)

    def chunk(k):
        stage(ra, z_r.at[0, k], k, sa)
        stage(rb, z_r.at[1, k], k, sb)

        def near(c, _):
            near_filter(c, g.at[k * CH + c], sa, sb, ya, yb, lhs_n, pa, pb)
            return 0

        lax.fori_loop(0, CH, near, 0)
        give(0, k, ya, ysa, 0)
        stage(rr, z_r.at[2, k], k, sr)

        def far(c, _):
            far_filter(c, g.at[k * CH + c], sr, yb, lhs_f, pf)
            return 0

        lax.fori_loop(0, CH, far, 0)
        give(1, k, yb, ysb, 0)

    chunk(0)

    def other(i, _):
        build_taps(hk.at[1], i * 64, g.at[CH + i])
        return 0

    lax.fori_loop(0, CH, other, 0)

    pltpu.make_async_copy(weight, wv, in_sem.at[3]).wait()
    for role in range(2):
        turned = h == 1 - role

        def gate_tile(i, _, role=role, turned=turned):
            col = pl.ds(pl.multiple_of(128 * i, 128), 128)
            o[role, :, col] = short(role, pl.ds(pl.multiple_of(128 * i + 2 * D, 128), 128))
            src = pl.multiple_of(jnp.where(turned, D // 128 - 1 - i, i) * 128, 128)
            wr[pl.ds(pl.multiple_of(role * D + 128 * i, 128), 128), :] = jnp.dot(
                flips[role], wv[pl.ds(src, 128), :], preferred_element_type=F32
            ).astype(BF16)
            return 0

        lax.fori_loop(0, D // 128, gate_tile, 0)

    chunk(1)

    straight = eye(False)
    for role in range(2):
        for k in range(2):
            half_rows = yt.at[role, pl.ds(0, D // 2)]
            pltpu.make_async_copy(half_rows, half_rows, y_r.at[role, k]).wait()
        for i in range(4):
            rows = pl.ds(256 * i, 256)
            y = lax.dot_general(
                straight, yt[role, rows, :], (((1,), (1,)), ((), ())), preferred_element_type=F32
            )
            c = (o[role, :, rows] * y).astype(BF16)
            cn[:, role * D + 256 * i : role * D + 256 * i + 256] = jnp.dot(
                flips[role], c, preferred_element_type=F32
            ).astype(BF16)
    for i in range(4):
        col = pl.ds(256 * i, 256)
        out[:, col] = jnp.dot(cn[...], wr[:, col], preferred_element_type=F32).astype(BF16)

    for k in range(2):
        for role in range(2):
            left = z.at[role, pl.ds(0, (NB - 1) * CH)]
            pltpu.make_async_copy(left, left, z_s.at[role, k]).wait()
            left = yt.at[role, pl.ds(0, (NB - 1) * CH)]
            pltpu.make_async_copy(left, left, y_s.at[role, k]).wait()
        left = z.at[0, pl.ds(0, NB * CH)]
        pltpu.make_async_copy(left, left, z_s.at[2, k]).wait()
    pltpu.make_async_copy(hsend.at[0], hsend.at[0], halo_s.at[0]).wait()

    @pl.when(slot > 0)
    def _():
        pltpu.make_async_copy(hsend.at[1], hsend.at[1], halo_s.at[1]).wait()

    def drain(i, _):
        pltpu.make_async_copy(piece(0, i), piece(0, i), up_s.at[i]).wait()
        pltpu.make_async_copy(piece(0, i), piece(0, i), dn_s.at[i]).wait()
        return 0

    lax.fori_loop(0, 8, drain, 0)


def per_device(fwd_proj, rev_proj, tokens, short_taps, long_kernel, skip_gain, out_weight):
    vmem = pltpu.VMEM
    dma = pltpu.SemaphoreType.DMA
    anywhere = pl.BlockSpec(memory_space=pl.ANY)
    local = pl.BlockSpec(memory_space=vmem)
    scratch = [
        vmem((2, POS, 3 * D), BF16),
        vmem((2, POS + 8, 3 * D), F32),
        vmem((2, 16, 3 * D), BF16),
        vmem((2, 16, 3 * D), BF16),
        vmem((2, D, POS), BF16),
        vmem((CH * 64, 128), F32),
        vmem((2, CH * 64, 128), BF16),
        vmem((2 * CH, 2048, 256), BF16),
        vmem((2, NB, CH, POS), BF16),
        vmem((2, NB, CH, POS), BF16),
        vmem((2, NB, CH, POS), BF16),
        vmem((SB * CH, 128), F32),
        vmem((SB * CH, 128), F32),
        vmem((SB * CH, 128), F32),
        vmem((NB * CH, 128), F32),
        vmem((NB * CH, 128), F32),
        vmem((2, NB, CH, POS), BF16),
        vmem((2, NB, CH, POS), BF16),
        vmem((2, D, POS), BF16),
        vmem((4 * NB, 1024), BF16),
        vmem((96, 2048), BF16),
        vmem((2, 8 + NB, 256), F32),
        vmem((2, 8 + NB, 256), F32),
        vmem((2, 48, 256), F32),
        vmem((2, POS, D), F32),
        vmem((D, D), BF16),
        vmem((2 * D, D), BF16),
        vmem((POS, 2 * D), BF16),
        vmem((CH, 8192), F32),
        dma((4,)),
        dma((2,)), dma((2,)),
        dma((8,)), dma((8,)), dma((8,)), dma((8,)),
        dma((3, 2)), dma((3, 2)),
        dma((2, 2)), dma((2, 2)),
    ]
    return pl.pallas_call(
        kernel,
        out_shape=jax.ShapeDtypeStruct((POS, D), BF16),
        in_specs=[anywhere, anywhere, local, local, anywhere, local, anywhere],
        out_specs=local,
        scratch_shapes=scratch,
        name="hyena",
        compiler_params=pltpu.CompilerParams(
            collective_id=0, has_side_effects=True, vmem_limit_bytes=60 * 2**20
        ),
    )(
        fwd_proj, rev_proj, tokens.reshape(1, POS), short_taps, long_kernel,
        skip_gain.reshape(CH, 1), out_weight,
    )


def solution(mesh):
    in_specs = (
        P(("dp", "ctx"), None),
        P(("dp", "ctx"), None),
        P(("dp", "ctx")),
        P(),
        P("ctx", None),
        P("ctx"),
        P(),
    )
    out_specs = P(("dp", "ctx"), None)
    return jax.shard_map(
        per_device, mesh=mesh, in_specs=in_specs, out_specs=out_specs, check_vma=False
    )
```

```python
import jax
import jax.numpy as jnp
from jax import lax
from jax.experimental import pallas as pl
from jax.experimental.pallas import tpu as pltpu
from jax.sharding import PartitionSpec as P

F32, BF16, I32 = jnp.float32, jnp.bfloat16, jnp.int32
MESH = pl.DeviceIdType.MESH
D = 1024
POS = 128
NB = 32
CH = 16
PAD = 16
ROWS = PAD + NB + PAD
LINE = 8
U = 4


def eye(flip):
    row = lax.broadcasted_iota(I32, (POS, POS), 0)
    col = lax.broadcasted_iota(I32, (POS, POS), 1)
    return (row == jnp.where(flip, POS - 1 - col, col)).astype(F32).astype(BF16)


def lane_below(rows, bound):
    return lax.broadcasted_iota(I32, (rows, 128), 1) < bound


def build_taps(rows_ref, first, count, out):
    row = lax.broadcasted_iota(I32, (8, 128), 0)
    lane = lax.broadcasted_iota(I32, (8, 128), 1)
    masks = [lane >= row + 8 * k for k in range(4)]
    before = [jnp.zeros((8, 128), F32)] * 4
    for j in range(count):
        if j % 16 == 0:
            rows = rows_ref[pl.ds(pl.multiple_of(first + j, 16), 16), :].astype(F32)
        wide = jnp.broadcast_to(rows[j % 16 : j % 16 + 1], (8, 128))
        now = [pltpu.roll(wide, 8 * k, 1, stride=1, stride_axis=0) for k in range(4)]
        at, col = 32 * (j // 2), 128 * (j % 2)
        for k in range(2):
            both = [jnp.where(masks[i], now[i], before[i]) for i in (2 * k, 2 * k + 1)]
            out[at + 16 * k : at + 16 * k + 16, col : col + 128] = jnp.concatenate(
                both, axis=0
            ).astype(BF16)
        before = now


def spread(staged, c, turned):
    x = staged[pl.ds(c, NB, stride=CH), :]
    turned[0, PAD : PAD + NB, :] = x
    for m in range(1, 4):
        turned[m, PAD : PAD + NB, :] = pltpu.roll(x, 32 * m, 1)


def pieces(turned, start, rows):
    for w in range(2):
        for rho in range(4):

            def load(i):
                return turned[(i - rho) % 4, pl.ds(PAD + start - 8 * w - 2 * i, rows), :]

            v = load(3)
            for i in (2, 1, 0):
                v = jnp.where(lane_below(rows, 32 * (i + 1)), load(i), v)
            yield w, rho, v.astype(BF16)


def overlap(part, at):
    def load(rho, off, col):
        return part[rho, pl.ds(at + off, NB), pl.ds(col, 128)]

    y = load(0, 0, 0) + load(0, -1, 128)
    for rho in range(1, 4):
        low = lane_below(NB, 32 * (4 - rho))
        mix = jnp.where(low, load(rho, 0, 0), load(rho, -1, 0)) + jnp.where(
            low, load(rho, -1, 128), load(rho, -2, 128)
        )
        y = y + pltpu.roll(mix, 32 * rho, 1)
    return y


def near_rows(c, sig_a, sig_b, lhs, turned):
    for which, staged in enumerate((sig_a, sig_b)):
        spread(staged, c, turned.at[which])
        for w, rho, v in pieces(turned.at[which], 0, NB):
            base = 4 * NB * which + NB * rho
            for s in range(2):
                lhs[base + 16 * s : base + NB, pl.ds(256 * s + 128 * w, 128)] = v[: NB - 16 * s]


def near_dot(taps, lhs, parts):
    acc = jnp.dot(lhs[...], taps[:512, :], preferred_element_type=F32)
    for i in range(2):
        for rho in range(4):
            at = (4 * i + rho) * NB
            parts[i, rho, 8 : 8 + NB, :] = acc[at : at + NB]


def near_sum(c, parts, out_a, out_b):
    at = pl.ds(c, NB, stride=CH)
    for i, out in enumerate((out_a, out_b)):
        out[at, :] = overlap(parts.at[i], 8)


def far_rows(c, sig, lhs, turned):
    spread(sig, c, turned)
    for w, rho, v in pieces(turned, -2, 48):
        for s in range(4):
            src = 32 - 16 * s
            dst = max(0, -src)
            src = max(0, src)
            count = min(48 - src, 48 - dst)
            at = 48 * rho + dst
            lhs[at : at + count, pl.ds(256 * s + 128 * w, 128)] = v[src : src + count]


def far_dot(taps, lhs, part):
    acc = jnp.dot(lhs[...], taps[...], preferred_element_type=F32)
    for rho in range(4):
        part[rho, :, :] = acc[48 * rho : 48 * rho + 48]


def far_sum(c, part, out, add):
    at = pl.ds(c, NB, stride=CH)
    y = overlap(part, 2)
    out[at, :] = out[at, :] + y if add else y


def kernel(
    fwd, rev, tok, taps, lk, skip, weight, out,
    xin, xf, hsend, halo, z, hf, hk, hn, ho, g, go, rab, rr, sa, sb, sr, ya, yb, ys, ps, yt, pt,
    o, comb, wv, lkv,
    ln0, ln1, ln2, ln3, lf0, lf1, lf2, lf3, tn0, tn1, tn2, tn3, pn0, pn1, pn2, pn3,
    pf0, pf1, pf2, pf3,
    in_sem, halo_s, halo_r, ex_s, ex_r, z_s, z_r, y_s, y_r,
):
    lns, lfs = (ln0, ln1, ln2, ln3), (lf0, lf1, lf2, lf3)
    tns, pns, pfs = (tn0, tn1, tn2, tn3), (pn0, pn1, pn2, pn3), (pf0, pf1, pf2, pf3)
    dp = lax.axis_index("dp")
    ctx = lax.axis_index("ctx")
    h = ctx // NB
    r = ctx - h * NB
    slot = jnp.where(h == 0, r, NB - 1 - r)
    quad = dp // 4
    seat = dp - 4 * quad
    across = (lax.rem(dp + 4, LINE), (1 - h) * NB + r)

    def mate(j):
        return (4 * quad + lax.rem(seat + j, 4), ctx)

    @pl.when(h == 0)
    def _():
        pltpu.make_async_copy(fwd, xin.at[0], in_sem.at[0]).start()
        pltpu.make_async_copy(rev, xin.at[1], in_sem.at[1]).start()

    @pl.when(h == 1)
    def _():
        pltpu.make_async_copy(rev, xin.at[0], in_sem.at[0]).start()
        pltpu.make_async_copy(fwd, xin.at[1], in_sem.at[1]).start()

    pltpu.make_async_copy(lk, lkv, in_sem.at[2]).start()
    pltpu.make_async_copy(weight, wv, in_sem.at[3]).start()

    barrier = pltpu.get_barrier_semaphore()

    def greet(who):
        pl.semaphore_signal(barrier, inc=1, device_id=who, device_id_type=MESH)

    greet(across)

    def greet_far(j, _):
        greet((dp, (1 - h) * NB + lax.rem(r + j, NB)))
        return 0

    def greet_near(j, _):
        greet((dp, h * NB + lax.rem(r + j, NB)))
        return 0

    lax.fori_loop(0, NB, greet_far, 0)
    for j in range(1, 4):
        greet(mate(j))
    lax.fori_loop(1, NB, greet_near, 0)

    for ref in lns + lfs + tns + pns:
        ref[...] = jnp.zeros_like(ref)

    flips = (eye(h == 1), eye(h == 0))
    for role in range(2):
        pltpu.make_async_copy(fwd, xin.at[role], in_sem.at[role]).wait()
        for i in range(6):
            col = pl.ds(512 * i, 512)
            x = jnp.dot(flips[role], xin[role, :, col], preferred_element_type=F32)
            xf[role, 8 : 8 + POS, col] = x
            hsend[role, :, col] = x[POS - 16 :].astype(BF16)

    pltpu.make_async_copy(lk, lkv, in_sem.at[2]).wait()
    diag = lax.broadcasted_iota(I32, (CH, CH), 0) == lax.broadcasted_iota(I32, (CH, CH), 1)
    gain = jnp.sum(jnp.where(diag, skip[...], 0.0), axis=1, keepdims=True)
    first = lax.broadcasted_iota(I32, (CH, 128), 1) == 0
    for j in range(64):
        v = lkv[:, 128 * j : 128 * j + 128]
        if j == 0:
            v = v + jnp.where(first, gain, 0.0)
        hf[pl.ds(j, CH, stride=64), :] = v
    for c in range(CH):
        v = hf[64 * c : 64 * c + 64, :].astype(BF16)
        hk[64 * c : 64 * c + 64, :] = v
        hn[32 * c : 32 * c + 32, :] = v[:32]

    pl.semaphore_wait(barrier, 2 * NB - 1 + 4)

    at_end = slot == NB - 1
    inner = jnp.where(h == 0, r + 1, r - 1)
    turn = jnp.where(h == 0, 0, NB - 1)
    next_a = jnp.where(at_end, (1 - h) * NB + turn, h * NB + inner)
    next_b = h * NB + jnp.where(h == 0, r - 1, r + 1)

    def halo_copy(src, dst, to):
        return pltpu.make_async_remote_copy(
            src_ref=hsend.at[src], dst_ref=halo.at[dst], send_sem=halo_s.at[src],
            recv_sem=halo_r.at[dst], device_id=(dp, to), device_id_type=MESH,
        )

    @pl.when(at_end)
    def _():
        halo_copy(0, 1, next_a).start()

    @pl.when(jnp.logical_not(at_end))
    def _():
        halo_copy(0, 0, next_a).start()

    @pl.when(slot > 0)
    def _():
        halo_copy(1, 1, next_b).start()

    share = pl.ds(pl.multiple_of(seat * 128, 128), 128)
    cross = pltpu.make_async_remote_copy(
        src_ref=hn.at[share], dst_ref=ho.at[share], send_sem=ex_s.at[0], recv_sem=ex_r.at[0],
        device_id=across, device_id_type=MESH,
    )
    cross.start()

    def own(i, _):
        for u in range(U):
            c = i * U + u
            build_taps(hk, c * 64, 64, g.at[c])
        return 0

    lax.fori_loop(0, CH // U, own, 0)

    known = (tok[...] != 4).astype(F32).astype(BF16)
    known = jnp.broadcast_to(known, (16, POS))

    def short(role, col):
        return (
            taps[0:1, col] * xf[role, 8 : 8 + POS, col]
            + taps[1:2, col] * xf[role, 7 : 7 + POS, col]
            + taps[2:3, col] * xf[role, 6 : 6 + POS, col]
        )

    def gate(role):
        mask = jnp.dot(known, flips[role], preferred_element_type=F32)[0:1]

        def tile(i, _):
            v = short(role, pl.ds(pl.multiple_of(128 * i, 128), 128))
            q = short(role, pl.ds(pl.multiple_of(128 * i + D, 128), 128))
            turned = (jnp.transpose(q * v) * mask).astype(BF16)
            z[pl.ds(8 * i, 8), role, :, :] = turned.reshape(8, CH, POS)
            return 0

        lax.fori_loop(0, D // 128, tile, 0)

    @pl.when(slot > 0)
    def _():
        pltpu.make_async_copy(halo.at[0], halo.at[0], halo_r.at[0]).wait()
        xf[0, 0:8, :] = halo[0, :, :].astype(F32)[8:16]

    @pl.when(slot == 0)
    def _():
        xf[0, 0:8, :] = jnp.zeros((8, 3 * D), F32)

    gate(0)

    def send_far(j, _):
        who = lax.rem(r + j, NB)
        pltpu.make_async_remote_copy(
            src_ref=z.at[(1 - h) * NB + who, 0], dst_ref=rr.at[slot],
            send_sem=z_s.at[2], recv_sem=z_r.at[2],
            device_id=(dp, (1 - h) * NB + who), device_id_type=MESH,
        ).start()
        return 0

    lax.fori_loop(0, NB, send_far, 0)

    pltpu.make_async_copy(halo.at[1], halo.at[1], halo_r.at[1]).wait()
    xf[1, 0:8, :] = halo[1, :, :].astype(F32)[8:16]
    gate(1)

    for k in range(2):
        group = h if k == 0 else 1 - h
        pltpu.make_async_copy(z.at[group * NB + r], rab.at[k, slot], z_r.at[k]).start()

        def send_near(j, _, k=k, group=group):
            who = lax.rem(r + j, NB)
            pltpu.make_async_remote_copy(
                src_ref=z.at[group * NB + who], dst_ref=rab.at[k, slot],
                send_sem=z_s.at[k], recv_sem=z_r.at[k],
                device_id=(dp, h * NB + who), device_id_type=MESH,
            ).start()
            return 0

        lax.fori_loop(1, NB, send_near, 0)

    cross.wait_recv()

    def mate_copy(j):
        return pltpu.make_async_remote_copy(
            src_ref=ho.at[share], dst_ref=ho.at[share], send_sem=ex_s.at[j],
            recv_sem=ex_r.at[j], device_id=mate(j), device_id_type=MESH,
        )

    for j in range(1, 4):
        mate_copy(j).start()

    for role in range(2):
        turned = h == 1 - role

        def gate_out(i, _, role=role, turned=turned):
            src = jnp.where(turned, D // 128 - 1 - i, i) * 128
            a = short(role, pl.ds(pl.multiple_of(src + 2 * D, 128), 128))
            high = a.astype(BF16)
            low = (a - high.astype(F32)).astype(BF16)
            both = jnp.concatenate([high, low], axis=1)
            both = jnp.dot(flips[role], both, preferred_element_type=F32).astype(BF16)
            both = jnp.concatenate([both[:, :128], both[:, 128:]], axis=0)
            both = jnp.dot(both, flips[role], preferred_element_type=F32)
            o[role, :, pl.ds(pl.multiple_of(128 * i, 128), 128)] = both[:POS] + both[POS:]
            return 0

        lax.fori_loop(0, D // 128, gate_out, 0)

    def stage(k):
        pltpu.make_async_copy(rab.at[k], rab.at[k], z_r.at[k]).wait()
        for b in range(NB):
            rows = pl.ds(CH * b, CH)
            sa[rows, :] = rab[k, b, 0, :, :].astype(F32)
            sb[rows, :] = rab[k, NB - 1 - b, 1, :, :].astype(F32)

    def near(taps_ref):
        def go(i, _):
            c = i * U
            for u in range(U):
                near_rows(c + u, sa, sb, lns[u], tns[u])
            for u in range(U):
                near_dot(taps_ref.at[c + u], lns[u], pns[u])
            for u in range(U):
                near_sum(c + u, pns[u], ya, yb)
            return 0

        lax.fori_loop(0, CH // U, go, 0)

    def far(sig, dst, add):
        def go(i, _):
            c = i * U
            for u in range(U):
                far_rows(c + u, sig, lfs[u], tns[u].at[0])
            for u in range(U):
                far_dot(g.at[c + u], lfs[u], pfs[u])
            for u in range(U):
                far_sum(c + u, pfs[u], dst, add)
            return 0

        lax.fori_loop(0, CH // U, go, 0)

    def pack_a(k):
        for b in range(NB):
            ys[k, b, 0, :, :] = ya[CH * b : CH * b + CH, :].astype(BF16)

    def pack_b(k):
        for b in range(NB):
            ys[k, NB - 1 - b, 1, :, :] = yb[CH * b : CH * b + CH, :].astype(BF16)

    def give(src, dst, sem):
        pltpu.make_async_copy(src(slot), dst, y_r.at[sem]).start()

        def go(j, _):
            who = lax.rem(r + j, NB)
            at = jnp.where(h == 0, who, NB - 1 - who)
            pltpu.make_async_remote_copy(
                src_ref=src(at), dst_ref=dst, send_sem=y_s.at[sem], recv_sem=y_r.at[sem],
                device_id=(dp, h * NB + who), device_id_type=MESH,
            ).start()
            return 0

        lax.fori_loop(1, NB, go, 0)

    stage(0)
    far(sa, yb, False)
    for b in range(NB):
        ps[b, :, :] = yb[CH * b : CH * b + CH, :].astype(BF16)

    def send_part(j, _):
        who = lax.rem(r + j, NB)
        at = jnp.where(h == 0, who, NB - 1 - who)
        pltpu.make_async_remote_copy(
            src_ref=ps.at[at], dst_ref=pt.at[r], send_sem=y_s.at[3], recv_sem=y_r.at[3],
            device_id=(dp, (1 - h) * NB + who), device_id_type=MESH,
        ).start()
        return 0

    lax.fori_loop(0, NB, send_part, 0)

    near(g)
    pack_a(0)
    give(lambda s: ys.at[0, s, 0], yt.at[h * NB + r, 0], 0)
    pltpu.make_async_copy(rr, rr, z_r.at[2]).wait()
    for b in range(NB):
        sr[CH * b : CH * b + CH, :] = rr[b, :, :].astype(F32)
    far(sr, yb, True)
    pack_b(0)
    give(lambda s: ys.at[0, s, 1], yt.at[h * NB + r, 1], 1)

    for j in range(1, 4):
        rows = pl.ds(pl.multiple_of(lax.rem(seat + 4 - j, 4) * 128, 128), 128)
        pltpu.make_async_copy(ho.at[rows], ho.at[rows], ex_r.at[j]).wait()

    def other(i, _):
        for u in range(U):
            c = i * U + u
            build_taps(ho, c * 32, 32, go.at[c])
        return 0

    lax.fori_loop(0, CH // U, other, 0)
    stage(1)
    near(go)
    pack_a(1)
    pack_b(1)
    give(lambda s: ys.at[1, s], yt.at[(1 - h) * NB + r], 2)

    def turn_back(role, y):
        y = lax.dot_general(
            flips[role], y, (((1,), (1,)), ((), ())), preferred_element_type=F32
        ).astype(BF16)
        return jnp.dot(y, flips[role], preferred_element_type=F32)

    def source(role, i):
        return jnp.where(h == 1 - role, D // 128 - 1 - i, i)

    own_rows = yt.at[pl.ds(0, NB), 0]
    both_rows = yt.at[pl.ds(0, NB)]
    pltpu.make_async_copy(own_rows, own_rows, y_r.at[0]).wait()
    pltpu.make_async_copy(both_rows, both_rows, y_r.at[2]).wait()
    for i in range(8):
        y = yt[pl.ds(8 * source(0, i), 8), 0, :, :].reshape(128, POS)
        col = pl.ds(128 * i, 128)
        o[0, :, col] = o[0, :, col] * turn_back(0, y)
    pltpu.make_async_copy(own_rows, own_rows, y_r.at[1]).wait()
    pltpu.make_async_copy(weight, wv, in_sem.at[3]).wait()
    pltpu.make_async_copy(pt, pt, y_r.at[3]).wait()
    mine = pl.ds((1 - h) * NB, NB)
    yt[mine, 1, :, :] = (yt[mine, 1, :, :].astype(F32) + pt[...].astype(F32)).astype(BF16)
    for i in range(8):
        y = yt[pl.ds(8 * source(1, i), 8), 1, :, :].reshape(128, POS)
        col = pl.ds(128 * i, 128)
        comb[:, col] = (o[0, :, col] + o[1, :, col] * turn_back(1, y)).astype(BF16)
    for i in range(4):
        col = pl.ds(256 * i, 256)
        out[:, col] = jnp.dot(comb[...], wv[:, col], preferred_element_type=F32).astype(BF16)

    for k in range(2):
        left = z.at[pl.ds(0, NB - 1)]
        pltpu.make_async_copy(left, left, z_s.at[k]).wait()
        left = yt.at[pl.ds(0, NB - 1), 0]
        pltpu.make_async_copy(left, left, y_s.at[k]).wait()
    left = z.at[pl.ds(0, NB), 0]
    pltpu.make_async_copy(left, left, z_s.at[2]).wait()
    left = yt.at[pl.ds(0, NB - 1)]
    pltpu.make_async_copy(left, left, y_s.at[2]).wait()
    pltpu.make_async_copy(ps, ps, y_s.at[3]).wait()
    cross.wait_send()
    for j in range(1, 4):
        mate_copy(j).wait_send()
    pltpu.make_async_copy(hsend.at[0], hsend.at[0], halo_s.at[0]).wait()

    @pl.when(slot > 0)
    def _():
        pltpu.make_async_copy(hsend.at[1], hsend.at[1], halo_s.at[1]).wait()


def per_device(fwd_proj, rev_proj, tokens, short_taps, long_kernel, skip_gain, out_weight):
    vmem = pltpu.VMEM
    dma = pltpu.SemaphoreType.DMA
    anywhere = pl.BlockSpec(memory_space=pl.ANY)
    local = pl.BlockSpec(memory_space=vmem)
    scratch = [
        vmem((2, POS, 3 * D), BF16),
        vmem((2, POS + 8, 3 * D), F32),
        vmem((2, 16, 3 * D), BF16),
        vmem((2, 16, 3 * D), BF16),
        vmem((D // CH, 2, CH, POS), BF16),
        vmem((CH * 64, 128), F32),
        vmem((CH * 64, 128), BF16),
        vmem((CH * 32, 128), BF16),
        vmem((CH * 32, 128), BF16),
        vmem((CH, 1024, 256), BF16),
        vmem((CH, 512, 256), BF16),
        vmem((2, NB, 2, CH, POS), BF16),
        vmem((NB, CH, POS), BF16),
        vmem((NB * CH, POS), F32),
        vmem((NB * CH, POS), F32),
        vmem((NB * CH, POS), F32),
        vmem((NB * CH, POS), F32),
        vmem((NB * CH, POS), F32),
        vmem((2, NB, 2, CH, POS), BF16),
        vmem((NB, CH, POS), BF16),
        vmem((D // CH, 2, CH, POS), BF16),
        vmem((NB, CH, POS), BF16),
        vmem((2, POS, D), F32),
        vmem((POS, D), BF16),
        vmem((D, D), BF16),
        vmem((CH, 8192), F32),
    ]
    scratch += [vmem((8 * NB, 512), BF16)] * U
    scratch += [vmem((4 * 48, 1024), BF16)] * U
    scratch += [vmem((2, 4, ROWS, 128), F32)] * U
    scratch += [vmem((2, 4, 8 + NB, 256), F32)] * U
    scratch += [vmem((4, 48, 256), F32)] * U
    scratch += [
        dma((4,)),
        dma((2,)), dma((2,)),
        dma((4,)), dma((4,)),
        dma((3,)), dma((3,)),
        dma((4,)), dma((4,)),
    ]
    return pl.pallas_call(
        kernel,
        out_shape=jax.ShapeDtypeStruct((POS, D), BF16),
        in_specs=[anywhere, anywhere, local, local, anywhere, local, anywhere],
        out_specs=local,
        scratch_shapes=scratch,
        name="hyena",
        compiler_params=pltpu.CompilerParams(
            collective_id=0, has_side_effects=True, vmem_limit_bytes=60 * 2**20
        ),
    )(
        fwd_proj, rev_proj, tokens.reshape(1, POS), short_taps, long_kernel,
        skip_gain.reshape(1, CH), out_weight,
    )


def solution(mesh):
    in_specs = (
        P(("dp", "ctx"), None),
        P(("dp", "ctx"), None),
        P(("dp", "ctx")),
        P(),
        P("ctx", None),
        P("ctx"),
        P(),
    )
    out_specs = P(("dp", "ctx"), None)
    return jax.shard_map(
        per_device, mesh=mesh, in_specs=in_specs, out_specs=out_specs, check_vma=False
    )
```

```python
import jax
import jax.numpy as jnp
from jax import lax
from jax.experimental import pallas as pl
from jax.experimental.pallas import tpu as pltpu
from jax.sharding import PartitionSpec as P

F32, BF16, I32 = jnp.float32, jnp.bfloat16, jnp.int32
MESH = pl.DeviceIdType.MESH
D = 1024
POS = 128
NB = 32
CH = 16
PAD = 16
ROWS = PAD + NB + PAD
LINE = 8
U = 4
TILES = 3 * D // 128


def eye(flip):
    row = lax.broadcasted_iota(I32, (POS, POS), 0)
    col = lax.broadcasted_iota(I32, (POS, POS), 1)
    return (row == jnp.where(flip, POS - 1 - col, col)).astype(F32).astype(BF16)


def lane_below(rows, bound):
    return lax.broadcasted_iota(I32, (rows, 128), 1) < bound


def build_taps(rows_ref, first, count, out):
    row = lax.broadcasted_iota(I32, (8, 128), 0)
    lane = lax.broadcasted_iota(I32, (8, 128), 1)
    masks = [lane >= row + 8 * k for k in range(4)]
    before = [jnp.zeros((8, 128), F32)] * 4
    for j in range(count):
        if j % 16 == 0:
            rows = rows_ref[pl.ds(pl.multiple_of(first + j, 16), 16), :].astype(F32)
        wide = jnp.broadcast_to(rows[j % 16 : j % 16 + 1], (8, 128))
        now = [pltpu.roll(wide, 8 * k, 1, stride=1, stride_axis=0) for k in range(4)]
        at, col = 32 * (j // 2), 128 * (j % 2)
        for k in range(2):
            both = [jnp.where(masks[i], now[i], before[i]) for i in (2 * k, 2 * k + 1)]
            out[at + 16 * k : at + 16 * k + 16, col : col + 128] = jnp.concatenate(
                both, axis=0
            ).astype(BF16)
        before = now


def spread(staged, c, turned):
    x = staged[pl.ds(c, NB, stride=CH), :]
    turned[0, PAD : PAD + NB, :] = x
    for m in range(1, 4):
        turned[m, PAD : PAD + NB, :] = pltpu.roll(x, 32 * m, 1)


def pieces(turned, start, rows):
    for rho in range(4):

        def load(i):
            return turned[(i - rho) % 4, pl.ds(PAD + start - 8 - 2 * i, rows + 8), :]

        v = load(3)
        for i in (2, 1, 0):
            v = jnp.where(lane_below(rows + 8, 32 * (i + 1)), load(i), v)
        for w in range(2):
            yield w, rho, v[8 - 8 * w : 8 - 8 * w + rows].astype(BF16)


def overlap(part, at):
    def load(rho, off, col):
        return part[rho, pl.ds(at + off, NB), pl.ds(col, 128)]

    y = load(0, 0, 0) + load(0, -1, 128)
    for rho in range(1, 4):
        low = lane_below(NB, 32 * (4 - rho))
        mix = jnp.where(low, load(rho, 0, 0), load(rho, -1, 0)) + jnp.where(
            low, load(rho, -1, 128), load(rho, -2, 128)
        )
        y = y + pltpu.roll(mix, 32 * rho, 1)
    return y


def near_rows(c, sig_a, sig_b, lhs, turned):
    for which, staged in enumerate((sig_a, sig_b)):
        spread(staged, c, turned.at[which])
        for w, rho, v in pieces(turned.at[which], 0, NB):
            base = 4 * NB * which + NB * rho
            for s in range(2):
                lhs[base + 16 * s : base + NB, pl.ds(256 * s + 128 * w, 128)] = v[: NB - 16 * s]


def near_dot(taps, lhs, parts):
    acc = jnp.dot(lhs[...], taps[:512, :], preferred_element_type=F32)
    for i in range(2):
        for rho in range(4):
            at = (4 * i + rho) * NB
            parts[i, rho, 8 : 8 + NB, :] = acc[at : at + NB]


def near_sum(c, parts, out_a, out_b):
    at = pl.ds(c, NB, stride=CH)
    for i, out in enumerate((out_a, out_b)):
        out[at, :] = overlap(parts.at[i], 8)


def far_rows(c, sig, lhs, turned):
    spread(sig, c, turned)
    for w, rho, v in pieces(turned, -2, 48):
        for s in range(4):
            src = 32 - 16 * s
            dst = max(0, -src)
            src = max(0, src)
            count = min(48 - src, 48 - dst)
            at = 48 * rho + dst
            lhs[at : at + count, pl.ds(256 * s + 128 * w, 128)] = v[src : src + count]


def far_dot(taps, lhs, part):
    acc = jnp.dot(lhs[...], taps[...], preferred_element_type=F32)
    for rho in range(4):
        part[rho, :, :] = acc[48 * rho : 48 * rho + 48]


def far_sum(c, part, out, add):
    at = pl.ds(c, NB, stride=CH)
    y = overlap(part, 2)
    out[at, :] = out[at, :] + y if add else y


def kernel(
    fwd, rev, tok, taps, lk, skip, weight, out,
    xin, xf, hs32, hsend, halo, hr32, z, hf, hk, hn, ho, g, go, rab, rr, sa, sb, sr, ya, yb, keep, ys, ps, yt, pt,
    o, comb, wv, lkv,
    ln0, ln1, ln2, ln3, lf0, lf1, lf2, lf3, tn0, tn1, tn2, tn3, pn0, pn1, pn2, pn3,
    pf0, pf1, pf2, pf3,
    in_sem, halo_s, halo_r, ex_s, ex_r, z_s, z_r, y_s, y_r,
):
    lns, lfs = (ln0, ln1, ln2, ln3), (lf0, lf1, lf2, lf3)
    tns, pns, pfs = (tn0, tn1, tn2, tn3), (pn0, pn1, pn2, pn3), (pf0, pf1, pf2, pf3)
    dp = lax.axis_index("dp")
    ctx = lax.axis_index("ctx")
    h = ctx // NB
    r = ctx - h * NB
    slot = jnp.where(h == 0, r, NB - 1 - r)
    quad = dp // 4
    seat = dp - 4 * quad
    across = (lax.rem(dp + 4, LINE), (1 - h) * NB + r)

    def mate(j):
        return (4 * quad + lax.rem(seat + j, 4), ctx)

    @pl.when(h == 0)
    def _():
        pltpu.make_async_copy(fwd, xin.at[0], in_sem.at[0]).start()
        pltpu.make_async_copy(rev, xin.at[1], in_sem.at[1]).start()

    @pl.when(h == 1)
    def _():
        pltpu.make_async_copy(rev, xin.at[0], in_sem.at[0]).start()
        pltpu.make_async_copy(fwd, xin.at[1], in_sem.at[1]).start()

    pltpu.make_async_copy(lk, lkv, in_sem.at[2]).start()
    pltpu.make_async_copy(weight, wv, in_sem.at[3]).start()

    barrier = pltpu.get_barrier_semaphore()

    def greet(who):
        pl.semaphore_signal(barrier, inc=1, device_id=who, device_id_type=MESH)

    greet(across)

    def greet_far(j, _):
        greet((dp, (1 - h) * NB + lax.rem(r + j, NB)))
        return 0

    def greet_near(j, _):
        greet((dp, h * NB + lax.rem(r + j, NB)))
        return 0

    lax.fori_loop(0, NB, greet_far, 0)
    for j in range(1, 4):
        greet(mate(j))
    lax.fori_loop(1, NB, greet_near, 0)

    flips = (eye(h == 1), eye(h == 0))

    def causal(role):
        pltpu.make_async_copy(fwd, xin.at[role], in_sem.at[role]).wait()
        for i in range(6):
            col = pl.ds(512 * i, 512)
            x = jnp.dot(flips[role], xin[role, :, col], preferred_element_type=F32)
            xf[role, 8 : 8 + POS, col] = x
        for t in range(TILES):
            hs32[role, 2 * t : 2 * t + 2, :] = xf[role, 6 + POS : 8 + POS, 128 * t : 128 * t + 128]
        hsend[role, :, :] = hs32[role, :, :].astype(BF16)

    causal(0)

    pl.semaphore_wait(barrier, 2 * NB - 1 + 4)

    at_end = slot == NB - 1
    inner = jnp.where(h == 0, r + 1, r - 1)
    turn = jnp.where(h == 0, 0, NB - 1)
    next_a = jnp.where(at_end, (1 - h) * NB + turn, h * NB + inner)
    next_b = h * NB + jnp.where(h == 0, r - 1, r + 1)

    def halo_copy(src, dst, to):
        return pltpu.make_async_remote_copy(
            src_ref=hsend.at[src], dst_ref=halo.at[dst], send_sem=halo_s.at[src],
            recv_sem=halo_r.at[dst], device_id=(dp, to), device_id_type=MESH,
        )

    @pl.when(at_end)
    def _():
        halo_copy(0, 1, next_a).start()

    @pl.when(jnp.logical_not(at_end))
    def _():
        halo_copy(0, 0, next_a).start()

    causal(1)

    @pl.when(slot > 0)
    def _():
        halo_copy(1, 1, next_b).start()

    pltpu.make_async_copy(lk, lkv, in_sem.at[2]).wait()
    diag = lax.broadcasted_iota(I32, (CH, CH), 0) == lax.broadcasted_iota(I32, (CH, CH), 1)
    gain = jnp.sum(jnp.where(diag, skip[...], 0.0), axis=1, keepdims=True)
    first = lax.broadcasted_iota(I32, (CH, 128), 1) == 0
    for j in range(64):
        v = lkv[:, 128 * j : 128 * j + 128]
        if j == 0:
            v = v + jnp.where(first, gain, 0.0)
        hf[pl.ds(j, CH, stride=64), :] = v
    for c in range(CH):
        v = hf[64 * c : 64 * c + 64, :].astype(BF16)
        hk[64 * c : 64 * c + 64, :] = v
        hn[32 * c : 32 * c + 32, :] = v[:32]

    share = pl.ds(pl.multiple_of(seat * 128, 128), 128)
    cross = pltpu.make_async_remote_copy(
        src_ref=hn.at[share], dst_ref=ho.at[share], send_sem=ex_s.at[0], recv_sem=ex_r.at[0],
        device_id=across, device_id_type=MESH,
    )
    cross.start()

    known = (tok[...] != 4).astype(F32).astype(BF16)
    known = jnp.broadcast_to(known, (16, POS))

    def short(role, col):
        return (
            taps[0:1, col] * xf[role, 8 : 8 + POS, col]
            + taps[1:2, col] * xf[role, 7 : 7 + POS, col]
            + taps[2:3, col] * xf[role, 6 : 6 + POS, col]
        )

    def gate(role):
        mask = jnp.dot(known, flips[role], preferred_element_type=F32)[0:1]

        def tile(i, _):
            for u in range(U):
                at = U * i + u
                v = short(role, pl.ds(pl.multiple_of(128 * at, 128), 128))
                q = short(role, pl.ds(pl.multiple_of(128 * at + D, 128), 128))
                turned = (jnp.transpose(q * v) * mask).astype(BF16)
                z[pl.ds(8 * at, 8), role, :, :] = turned.reshape(8, CH, POS)
            return 0

        lax.fori_loop(0, D // 128 // U, tile, 0)

    def before(role):
        pltpu.make_async_copy(halo.at[role], halo.at[role], halo_r.at[role]).wait()
        hr32[role, :, :] = halo[role, :, :].astype(F32)
        for t in range(TILES):
            xf[role, 6:8, 128 * t : 128 * t + 128] = hr32[role, 2 * t : 2 * t + 2, :]

    @pl.when(slot > 0)
    def _():
        before(0)

    @pl.when(slot == 0)
    def _():
        xf[0, 0:8, :] = jnp.zeros((8, 3 * D), F32)

    gate(0)

    def send_far(j, _):
        who = lax.rem(r + j, NB)
        pltpu.make_async_remote_copy(
            src_ref=z.at[(1 - h) * NB + who, 0], dst_ref=rr.at[slot],
            send_sem=z_s.at[2], recv_sem=z_r.at[2],
            device_id=(dp, (1 - h) * NB + who), device_id_type=MESH,
        ).start()
        return 0


    def send_near(src, dst, sem):
        pltpu.make_async_copy(src(r), dst, z_r.at[sem]).start()

        def go(j, _):
            who = lax.rem(r + j, NB)
            pltpu.make_async_remote_copy(
                src_ref=src(who), dst_ref=dst, send_sem=z_s.at[sem], recv_sem=z_r.at[sem],
                device_id=(dp, h * NB + who), device_id_type=MESH,
            ).start()
            return 0

        lax.fori_loop(1, NB, go, 0)

    send_near(lambda who: z.at[h * NB + who, 0], rab.at[0, slot, 0], 0)
    lax.fori_loop(0, NB, send_far, 0)
    cross.wait_recv()

    def mate_copy(j):
        return pltpu.make_async_remote_copy(
            src_ref=ho.at[share], dst_ref=ho.at[share], send_sem=ex_s.at[j],
            recv_sem=ex_r.at[j], device_id=mate(j), device_id_type=MESH,
        )

    for j in range(1, 4):
        mate_copy(j).start()

    before(1)
    gate(1)
    send_near(lambda who: z.at[h * NB + who, 1], rab.at[0, slot, 1], 3)
    send_near(lambda who: z.at[(1 - h) * NB + who], rab.at[1, slot], 1)

    for ref in lns + lfs + tns + pns:
        ref[...] = jnp.zeros_like(ref)

    def own(i, _):
        for u in range(U):
            c = i * U + u
            build_taps(hk, c * 64, 64, g.at[c])
        return 0

    lax.fori_loop(0, CH // U, own, 0)

    for role in range(2):
        turned = h == 1 - role

        for i in range(D // 128):
            src = jnp.where(turned, D // 128 - 1 - i, i) * 128
            a = short(role, pl.ds(pl.multiple_of(src + 2 * D, 128), 128))
            high = a.astype(BF16)
            low = (a - high.astype(F32)).astype(BF16)
            both = jnp.concatenate([high, low], axis=1)
            both = jnp.dot(flips[role], both, preferred_element_type=F32).astype(BF16)
            both = jnp.concatenate([both[:, :128], both[:, 128:]], axis=0)
            both = jnp.dot(both, flips[role], preferred_element_type=F32)
            o[role, :, 128 * i : 128 * i + 128] = both[:POS] + both[POS:]

    def stage_a(k):
        for b in range(NB):
            sa[CH * b : CH * b + CH, :] = rab[k, b, 0, :, :].astype(F32)

    def stage_b(k):
        for b in range(NB):
            sb[CH * b : CH * b + CH, :] = rab[k, NB - 1 - b, 1, :, :].astype(F32)

    def near(taps_ref):
        def go(i, _):
            c = i * U
            for u in range(U):
                near_rows(c + u, sa, sb, lns[u], tns[u])
            for u in range(U):
                near_dot(taps_ref.at[c + u], lns[u], pns[u])
            for u in range(U):
                near_sum(c + u, pns[u], ya, yb)
            return 0

        lax.fori_loop(0, CH // U, go, 0)

    def far(sig, dst, add):
        def go(i, _):
            c = i * U
            for u in range(U):
                far_rows(c + u, sig, lfs[u], tns[u].at[0])
            for u in range(U):
                far_dot(g.at[c + u], lfs[u], pfs[u])
            for u in range(U):
                far_sum(c + u, pfs[u], dst, add)
            return 0

        lax.fori_loop(0, CH // U, go, 0)

    def pack_a(k):
        for b in range(NB):
            ys[k, b, 0, :, :] = ya[CH * b : CH * b + CH, :].astype(BF16)

    def pack_b(k, src):
        for b in range(NB):
            ys[k, NB - 1 - b, 1, :, :] = src[CH * b : CH * b + CH, :].astype(BF16)

    def give(src, dst, sem):
        pltpu.make_async_copy(src(slot), dst, y_r.at[sem]).start()

        def go(j, _):
            who = lax.rem(r + j, NB)
            at = jnp.where(h == 0, who, NB - 1 - who)
            pltpu.make_async_remote_copy(
                src_ref=src(at), dst_ref=dst, send_sem=y_s.at[sem], recv_sem=y_r.at[sem],
                device_id=(dp, h * NB + who), device_id_type=MESH,
            ).start()
            return 0

        lax.fori_loop(1, NB, go, 0)

    half_of = rab.at[0, pl.ds(0, NB), 0]
    pltpu.make_async_copy(half_of, half_of, z_r.at[0]).wait()
    stage_a(0)
    far(sa, yb, False)
    for b in range(NB):
        ps[b, :, :] = yb[CH * b : CH * b + CH, :].astype(BF16)

    def send_part(j, _):
        who = lax.rem(r + j, NB)
        at = jnp.where(h == 0, who, NB - 1 - who)
        pltpu.make_async_remote_copy(
            src_ref=ps.at[at], dst_ref=pt.at[r], send_sem=y_s.at[3], recv_sem=y_r.at[3],
            device_id=(dp, (1 - h) * NB + who), device_id_type=MESH,
        ).start()
        return 0

    lax.fori_loop(0, NB, send_part, 0)

    pltpu.make_async_copy(half_of, half_of, z_r.at[3]).wait()
    stage_b(0)
    near(g)
    pack_a(0)
    give(lambda at: ys.at[0, at, 0], yt.at[h * NB + r, 0], 0)
    keep[...] = yb[...]

    for j in range(1, 4):
        rows = pl.ds(pl.multiple_of(lax.rem(seat + 4 - j, 4) * 128, 128), 128)
        pltpu.make_async_copy(ho.at[rows], ho.at[rows], ex_r.at[j]).wait()

    def other(i, _):
        for u in range(U):
            c = i * U + u
            build_taps(ho, c * 32, 32, go.at[c])
        return 0

    lax.fori_loop(0, CH // U, other, 0)
    pltpu.make_async_copy(rab.at[1], rab.at[1], z_r.at[1]).wait()
    stage_a(1)
    stage_b(1)
    near(go)
    pack_a(1)
    pack_b(1, yb)
    give(lambda at: ys.at[1, at], yt.at[(1 - h) * NB + r], 2)

    pltpu.make_async_copy(rr, rr, z_r.at[2]).wait()
    for b in range(NB):
        sr[CH * b : CH * b + CH, :] = rr[b, :, :].astype(F32)
    far(sr, keep, True)
    pack_b(0, keep)
    give(lambda at: ys.at[0, at, 1], yt.at[h * NB + r, 1], 1)

    def turn_back(role, y):
        y = lax.dot_general(
            flips[role], y, (((1,), (1,)), ((), ())), preferred_element_type=F32
        ).astype(BF16)
        return jnp.dot(y, flips[role], preferred_element_type=F32)

    def source(role, i):
        return jnp.where(h == 1 - role, D // 128 - 1 - i, i)

    own_rows = yt.at[pl.ds(0, NB), 0]
    both_rows = yt.at[pl.ds(0, NB)]
    pltpu.make_async_copy(own_rows, own_rows, y_r.at[0]).wait()
    pltpu.make_async_copy(both_rows, both_rows, y_r.at[2]).wait()
    for i in range(8):
        y = yt[pl.ds(8 * source(0, i), 8), 0, :, :].reshape(128, POS)
        col = pl.ds(128 * i, 128)
        o[0, :, col] = o[0, :, col] * turn_back(0, y)
    def add_strand(i):
        y = yt[pl.ds(8 * source(1, i), 8), 1, :, :].reshape(128, POS)
        col = pl.ds(128 * i, 128)
        comb[:, col] = (o[0, :, col] + o[1, :, col] * turn_back(1, y)).astype(BF16)

    def project(rows, col):
        return jnp.dot(comb[:, rows], wv[rows, col], preferred_element_type=F32)

    pltpu.make_async_copy(weight, wv, in_sem.at[3]).wait()
    pltpu.make_async_copy(own_rows, own_rows, y_r.at[1]).wait()
    for i in range(4, 8):
        add_strand(i)
    for i in range(4):
        col = pl.ds(256 * i, 256)
        o[0, :, col] = project(pl.ds(D // 2, D // 2), col) if i >= 2 else o[0, :, col]
    pltpu.make_async_copy(pt, pt, y_r.at[3]).wait()
    mine = pl.ds((1 - h) * NB, NB)
    yt[mine, 1, :, :] = (yt[mine, 1, :, :].astype(F32) + pt[...].astype(F32)).astype(BF16)
    for i in range(4):
        add_strand(i)
    for i in range(4):
        col = pl.ds(256 * i, 256)
        if i >= 2:
            total = o[0, :, col] + project(pl.ds(0, D // 2), col)
        else:
            total = project(pl.ds(0, D), col)
        out[:, col] = total.astype(BF16)

    for k in range(2):
        left = yt.at[pl.ds(0, NB - 1), 0]
        pltpu.make_async_copy(left, left, z_s.at[3 * k]).wait()
        pltpu.make_async_copy(left, left, y_s.at[k]).wait()
    left = z.at[pl.ds(0, NB - 1)]
    pltpu.make_async_copy(left, left, z_s.at[1]).wait()
    left = z.at[pl.ds(0, NB), 0]
    pltpu.make_async_copy(left, left, z_s.at[2]).wait()
    left = yt.at[pl.ds(0, NB - 1)]
    pltpu.make_async_copy(left, left, y_s.at[2]).wait()
    pltpu.make_async_copy(ps, ps, y_s.at[3]).wait()
    cross.wait_send()
    for j in range(1, 4):
        mate_copy(j).wait_send()
    pltpu.make_async_copy(hsend.at[0], hsend.at[0], halo_s.at[0]).wait()

    @pl.when(slot > 0)
    def _():
        pltpu.make_async_copy(hsend.at[1], hsend.at[1], halo_s.at[1]).wait()


def per_device(fwd_proj, rev_proj, tokens, short_taps, long_kernel, skip_gain, out_weight):
    vmem = pltpu.VMEM
    dma = pltpu.SemaphoreType.DMA
    anywhere = pl.BlockSpec(memory_space=pl.ANY)
    local = pl.BlockSpec(memory_space=vmem)
    scratch = [
        vmem((2, POS, 3 * D), BF16),
        vmem((2, POS + 8, 3 * D), F32),
        vmem((2, 2 * TILES, 128), F32),
        vmem((2, 2 * TILES, 128), BF16),
        vmem((2, 2 * TILES, 128), BF16),
        vmem((2, 2 * TILES, 128), F32),
        vmem((D // CH, 2, CH, POS), BF16),
        vmem((CH * 64, 128), F32),
        vmem((CH * 64, 128), BF16),
        vmem((CH * 32, 128), BF16),
        vmem((CH * 32, 128), BF16),
        vmem((CH, 1024, 256), BF16),
        vmem((CH, 512, 256), BF16),
        vmem((2, NB, 2, CH, POS), BF16),
        vmem((NB, CH, POS), BF16),
        vmem((NB * CH, POS), F32),
        vmem((NB * CH, POS), F32),
        vmem((NB * CH, POS), F32),
        vmem((NB * CH, POS), F32),
        vmem((NB * CH, POS), F32),
        vmem((NB * CH, POS), F32),
        vmem((2, NB, 2, CH, POS), BF16),
        vmem((NB, CH, POS), BF16),
        vmem((D // CH, 2, CH, POS), BF16),
        vmem((NB, CH, POS), BF16),
        vmem((2, POS, D), F32),
        vmem((POS, D), BF16),
        vmem((D, D), BF16),
        vmem((CH, 8192), F32),
    ]
    scratch += [vmem((8 * NB, 512), BF16)] * U
    scratch += [vmem((4 * 48, 1024), BF16)] * U
    scratch += [vmem((2, 4, ROWS, 128), F32)] * U
    scratch += [vmem((2, 4, 8 + NB, 256), F32)] * U
    scratch += [vmem((4, 48, 256), F32)] * U
    scratch += [
        dma((4,)),
        dma((2,)), dma((2,)),
        dma((4,)), dma((4,)),
        dma((4,)), dma((4,)),
        dma((4,)), dma((4,)),
    ]
    return pl.pallas_call(
        kernel,
        out_shape=jax.ShapeDtypeStruct((POS, D), BF16),
        in_specs=[anywhere, anywhere, local, local, anywhere, local, anywhere],
        out_specs=local,
        scratch_shapes=scratch,
        name="hyena",
        compiler_params=pltpu.CompilerParams(
            collective_id=0, has_side_effects=True, vmem_limit_bytes=60 * 2**20
        ),
    )(
        fwd_proj, rev_proj, tokens.reshape(1, POS), short_taps, long_kernel,
        skip_gain.reshape(1, CH), out_weight,
    )


def solution(mesh):
    in_specs = (
        P(("dp", "ctx"), None),
        P(("dp", "ctx"), None),
        P(("dp", "ctx")),
        P(),
        P("ctx", None),
        P("ctx"),
        P(),
    )
    out_specs = P(("dp", "ctx"), None)
    return jax.shard_map(
        per_device, mesh=mesh, in_specs=in_specs, out_specs=out_specs, check_vma=False
    )
```

```python
import jax
import jax.numpy as jnp
from jax import lax
from jax.experimental import pallas as pl
from jax.experimental.pallas import tpu as pltpu
from jax.sharding import PartitionSpec as P

F32, BF16, I32 = jnp.float32, jnp.bfloat16, jnp.int32
MESH = pl.DeviceIdType.MESH
D = 1024
POS = 128
NB = 32
CH = 16
PAD = 16
ROWS = PAD + NB + PAD
LINE = 8
U = 4
W = 16
TILES = 3 * D // 128


def eye(flip):
    row = lax.broadcasted_iota(I32, (POS, POS), 0)
    col = lax.broadcasted_iota(I32, (POS, POS), 1)
    return (row == jnp.where(flip, POS - 1 - col, col)).astype(F32).astype(BF16)


def lane_below(rows, bound):
    return lax.broadcasted_iota(I32, (rows, 128), 1) < bound


def build_taps(rows_ref, first, count, out):
    row = lax.broadcasted_iota(I32, (8, 128), 0)
    lane = lax.broadcasted_iota(I32, (8, 128), 1)
    masks = [lane >= row + 8 * k for k in range(4)]
    before = [jnp.zeros((8, 128), F32)] * 4
    for j in range(count):
        if j % 16 == 0:
            rows = rows_ref[pl.ds(pl.multiple_of(first + j, 16), 16), :].astype(F32)
        wide = jnp.broadcast_to(rows[j % 16 : j % 16 + 1], (8, 128))
        now = [pltpu.roll(wide, 8 * k, 1, stride=1, stride_axis=0) for k in range(4)]
        at, col = 32 * (j // 2), 128 * (j % 2)
        for k in range(2):
            both = [jnp.where(masks[i], now[i], before[i]) for i in (2 * k, 2 * k + 1)]
            out[at + 16 * k : at + 16 * k + 16, col : col + 128] = jnp.concatenate(
                both, axis=0
            ).astype(BF16)
        before = now


def spread(staged, c, turned):
    x = staged[pl.ds(c, NB, stride=CH), :]
    turned[0, PAD : PAD + NB, :] = x
    for m in range(1, 4):
        turned[m, PAD : PAD + NB, :] = pltpu.roll(x, 32 * m, 1)


def pieces(turned, start, rows):
    for rho in range(4):

        def load(i):
            return turned[(i - rho) % 4, pl.ds(PAD + start - 8 - 2 * i, rows + 8), :]

        v = load(3)
        for i in (2, 1, 0):
            v = jnp.where(lane_below(rows + 8, 32 * (i + 1)), load(i), v)
        for w in range(2):
            yield w, rho, v[8 - 8 * w : 8 - 8 * w + rows].astype(BF16)


def overlap(part, at):
    def load(rho, off, col):
        return part[rho, pl.ds(at + off, NB), pl.ds(col, 128)]

    y = load(0, 0, 0) + load(0, -1, 128)
    for rho in range(1, 4):
        low = lane_below(NB, 32 * (4 - rho))
        mix = jnp.where(low, load(rho, 0, 0), load(rho, -1, 0)) + jnp.where(
            low, load(rho, -1, 128), load(rho, -2, 128)
        )
        y = y + pltpu.roll(mix, 32 * rho, 1)
    return y


def near_rows(c, sig_a, sig_b, lhs, turned):
    for which, staged in enumerate((sig_a, sig_b)):
        spread(staged, c, turned.at[which])
        for w, rho, v in pieces(turned.at[which], 0, NB):
            base = 4 * NB * which + NB * rho
            for s in range(2):
                lhs[base + 16 * s : base + NB, pl.ds(256 * s + 128 * w, 128)] = v[: NB - 16 * s]


def near_dot(taps, lhs, parts):
    acc = jnp.dot(lhs[...], taps[:512, :], preferred_element_type=F32)
    for i in range(2):
        for rho in range(4):
            at = (4 * i + rho) * NB
            parts[i, rho, 8 : 8 + NB, :] = acc[at : at + NB]


def near_sum(c, parts, out_a, out_b):
    at = pl.ds(c, NB, stride=CH)
    for i, out in enumerate((out_a, out_b)):
        out[at, :] = overlap(parts.at[i], 8)


def far_rows(c, sig, lhs, turned):
    spread(sig, c, turned)
    for w, rho, v in pieces(turned, -2, 48):
        for s in range(4):
            src = 32 - 16 * s
            dst = max(0, -src)
            src = max(0, src)
            count = min(48 - src, 48 - dst)
            at = 48 * rho + dst
            lhs[at : at + count, pl.ds(256 * s + 128 * w, 128)] = v[src : src + count]


def far_dot(taps, lhs, part):
    acc = jnp.dot(lhs[...], taps[...], preferred_element_type=F32)
    for rho in range(4):
        part[rho, :, :] = acc[48 * rho : 48 * rho + 48]


def far_sum(c, part, out, add):
    at = pl.ds(c, NB, stride=CH)
    y = overlap(part, 2)
    out[at, :] = out[at, :] + y if add else y


def kernel(
    fwd, rev, tok, taps, lk, skip, weight, out,
    xin, xf, hs32, hsend, halo, hr32, z, hf, hk, hn, ho, g, go, rab, rr, sa, sb, sr, ya, yb, keep, ys, ps, yt, pt,
    o, comb, wv, lkv,
    *rest,
):
    lns, lfs, tns, pns, pfs = (rest[W * i : W * i + W] for i in range(5))
    in_sem, halo_s, halo_r, ex_s, ex_r, z_s, z_r, y_s, y_r = rest[5 * W :]
    dp = lax.axis_index("dp")
    ctx = lax.axis_index("ctx")
    h = ctx // NB
    r = ctx - h * NB
    slot = jnp.where(h == 0, r, NB - 1 - r)
    quad = dp // 4
    seat = dp - 4 * quad
    across = (lax.rem(dp + 4, LINE), (1 - h) * NB + r)

    def mate(j):
        return (4 * quad + lax.rem(seat + j, 4), ctx)

    @pl.when(h == 0)
    def _():
        pltpu.make_async_copy(fwd, xin.at[0], in_sem.at[0]).start()
        pltpu.make_async_copy(rev, xin.at[1], in_sem.at[1]).start()

    @pl.when(h == 1)
    def _():
        pltpu.make_async_copy(rev, xin.at[0], in_sem.at[0]).start()
        pltpu.make_async_copy(fwd, xin.at[1], in_sem.at[1]).start()

    pltpu.make_async_copy(lk, lkv, in_sem.at[2]).start()
    pltpu.make_async_copy(weight, wv, in_sem.at[3]).start()

    barrier = pltpu.get_barrier_semaphore()

    def greet(who):
        pl.semaphore_signal(barrier, inc=1, device_id=who, device_id_type=MESH)

    greet(across)

    def greet_far(j, _):
        greet((dp, (1 - h) * NB + lax.rem(r + j, NB)))
        return 0

    def greet_near(j, _):
        greet((dp, h * NB + lax.rem(r + j, NB)))
        return 0

    lax.fori_loop(0, NB, greet_far, 0)
    for j in range(1, 4):
        greet(mate(j))
    lax.fori_loop(1, NB, greet_near, 0)

    flips = (eye(h == 1), eye(h == 0))

    def causal(role):
        pltpu.make_async_copy(fwd, xin.at[role], in_sem.at[role]).wait()
        for i in range(6):
            col = pl.ds(512 * i, 512)
            x = jnp.dot(flips[role], xin[role, :, col], preferred_element_type=F32)
            xf[role, 8 : 8 + POS, col] = x
        for t in range(TILES):
            hs32[role, 2 * t : 2 * t + 2, :] = xf[role, 6 + POS : 8 + POS, 128 * t : 128 * t + 128]
        hsend[role, :, :] = hs32[role, :, :].astype(BF16)

    causal(0)

    pl.semaphore_wait(barrier, 2 * NB - 1 + 4)

    at_end = slot == NB - 1
    inner = jnp.where(h == 0, r + 1, r - 1)
    turn = jnp.where(h == 0, 0, NB - 1)
    next_a = jnp.where(at_end, (1 - h) * NB + turn, h * NB + inner)
    next_b = h * NB + jnp.where(h == 0, r - 1, r + 1)

    def halo_copy(src, dst, to):
        return pltpu.make_async_remote_copy(
            src_ref=hsend.at[src], dst_ref=halo.at[dst], send_sem=halo_s.at[src],
            recv_sem=halo_r.at[dst], device_id=(dp, to), device_id_type=MESH,
        )

    @pl.when(at_end)
    def _():
        halo_copy(0, 1, next_a).start()

    @pl.when(jnp.logical_not(at_end))
    def _():
        halo_copy(0, 0, next_a).start()

    causal(1)

    @pl.when(slot > 0)
    def _():
        halo_copy(1, 1, next_b).start()

    pltpu.make_async_copy(lk, lkv, in_sem.at[2]).wait()
    diag = lax.broadcasted_iota(I32, (CH, CH), 0) == lax.broadcasted_iota(I32, (CH, CH), 1)
    gain = jnp.sum(jnp.where(diag, skip[...], 0.0), axis=1, keepdims=True)
    first = lax.broadcasted_iota(I32, (CH, 128), 1) == 0
    for j in range(64):
        v = lkv[:, 128 * j : 128 * j + 128]
        if j == 0:
            v = v + jnp.where(first, gain, 0.0)
        hf[pl.ds(j, CH, stride=64), :] = v
    for c in range(CH):
        v = hf[64 * c : 64 * c + 64, :].astype(BF16)
        hk[64 * c : 64 * c + 64, :] = v
        hn[32 * c : 32 * c + 32, :] = v[:32]

    share = pl.ds(pl.multiple_of(seat * 128, 128), 128)
    cross = pltpu.make_async_remote_copy(
        src_ref=hn.at[share], dst_ref=ho.at[share], send_sem=ex_s.at[0], recv_sem=ex_r.at[0],
        device_id=across, device_id_type=MESH,
    )
    cross.start()

    known = (tok[...] != 4).astype(F32).astype(BF16)
    known = jnp.broadcast_to(known, (16, POS))

    def short(role, col):
        return (
            taps[0:1, col] * xf[role, 8 : 8 + POS, col]
            + taps[1:2, col] * xf[role, 7 : 7 + POS, col]
            + taps[2:3, col] * xf[role, 6 : 6 + POS, col]
        )

    def gate(role):
        mask = jnp.dot(known, flips[role], preferred_element_type=F32)[0:1]

        def tile(i, _):
            for u in range(U):
                at = U * i + u
                v = short(role, pl.ds(pl.multiple_of(128 * at, 128), 128))
                q = short(role, pl.ds(pl.multiple_of(128 * at + D, 128), 128))
                turned = (jnp.transpose(q * v) * mask).astype(BF16)
                z[pl.ds(8 * at, 8), role, :, :] = turned.reshape(8, CH, POS)
            return 0

        lax.fori_loop(0, D // 128 // U, tile, 0)

    def before(role):
        pltpu.make_async_copy(halo.at[role], halo.at[role], halo_r.at[role]).wait()
        hr32[role, :, :] = halo[role, :, :].astype(F32)
        for t in range(TILES):
            xf[role, 6:8, 128 * t : 128 * t + 128] = hr32[role, 2 * t : 2 * t + 2, :]

    @pl.when(slot > 0)
    def _():
        before(0)

    @pl.when(slot == 0)
    def _():
        xf[0, 0:8, :] = jnp.zeros((8, 3 * D), F32)

    gate(0)

    def send_far(j, _):
        who = lax.rem(r + j, NB)
        pltpu.make_async_remote_copy(
            src_ref=z.at[(1 - h) * NB + who, 0], dst_ref=rr.at[slot],
            send_sem=z_s.at[2], recv_sem=z_r.at[2],
            device_id=(dp, (1 - h) * NB + who), device_id_type=MESH,
        ).start()
        return 0


    def send_near(src, dst, sem):
        pltpu.make_async_copy(src(r), dst, z_r.at[sem]).start()

        def go(j, _):
            who = lax.rem(r + j, NB)
            pltpu.make_async_remote_copy(
                src_ref=src(who), dst_ref=dst, send_sem=z_s.at[sem], recv_sem=z_r.at[sem],
                device_id=(dp, h * NB + who), device_id_type=MESH,
            ).start()
            return 0

        lax.fori_loop(1, NB, go, 0)

    send_near(lambda who: z.at[h * NB + who, 0], rab.at[0, slot, 0], 0)
    lax.fori_loop(0, NB, send_far, 0)
    cross.wait_recv()

    def mate_copy(j):
        return pltpu.make_async_remote_copy(
            src_ref=ho.at[share], dst_ref=ho.at[share], send_sem=ex_s.at[j],
            recv_sem=ex_r.at[j], device_id=mate(j), device_id_type=MESH,
        )

    for j in range(1, 4):
        mate_copy(j).start()

    before(1)
    gate(1)
    send_near(lambda who: z.at[h * NB + who, 1], rab.at[0, slot, 1], 3)
    send_near(lambda who: z.at[(1 - h) * NB + who], rab.at[1, slot], 1)

    for ref in lns + lfs + tns + pns:
        ref[...] = jnp.zeros_like(ref)

    def own(i, _):
        for u in range(U):
            c = i * U + u
            build_taps(hk, c * 64, 64, g.at[c])
        return 0

    lax.fori_loop(0, CH // U, own, 0)

    for role in range(2):
        turned = h == 1 - role

        for i in range(D // 128):
            src = jnp.where(turned, D // 128 - 1 - i, i) * 128
            a = short(role, pl.ds(pl.multiple_of(src + 2 * D, 128), 128))
            high = a.astype(BF16)
            low = (a - high.astype(F32)).astype(BF16)
            both = jnp.concatenate([high, low], axis=1)
            both = jnp.dot(flips[role], both, preferred_element_type=F32).astype(BF16)
            both = jnp.concatenate([both[:, :128], both[:, 128:]], axis=0)
            both = jnp.dot(both, flips[role], preferred_element_type=F32)
            o[role, :, 128 * i : 128 * i + 128] = both[:POS] + both[POS:]

    def stage_a(k):
        for b in range(NB):
            sa[CH * b : CH * b + CH, :] = rab[k, b, 0, :, :].astype(F32)

    def stage_b(k):
        for b in range(NB):
            sb[CH * b : CH * b + CH, :] = rab[k, NB - 1 - b, 1, :, :].astype(F32)

    def near(taps_ref):
        def go(i, _):
            c = i * W
            for u in range(W):
                near_rows(c + u, sa, sb, lns[u], tns[u])
            for u in range(W):
                near_dot(taps_ref.at[c + u], lns[u], pns[u])
            for u in range(W):
                near_sum(c + u, pns[u], ya, yb)
            return 0

        go(0, 0)

    def far(sig, dst, add):
        def go(i, _):
            c = i * W
            for u in range(W):
                far_rows(c + u, sig, lfs[u], tns[u].at[0])
            for u in range(W):
                far_dot(g.at[c + u], lfs[u], pfs[u])
            for u in range(W):
                far_sum(c + u, pfs[u], dst, add)
            return 0

        go(0, 0)

    def pack_a(k):
        for b in range(NB):
            ys[k, b, 0, :, :] = ya[CH * b : CH * b + CH, :].astype(BF16)

    def pack_b(k, src):
        for b in range(NB):
            ys[k, NB - 1 - b, 1, :, :] = src[CH * b : CH * b + CH, :].astype(BF16)

    def give(src, dst, sem):
        pltpu.make_async_copy(src(slot), dst, y_r.at[sem]).start()

        def go(j, _):
            who = lax.rem(r + j, NB)
            at = jnp.where(h == 0, who, NB - 1 - who)
            pltpu.make_async_remote_copy(
                src_ref=src(at), dst_ref=dst, send_sem=y_s.at[sem], recv_sem=y_r.at[sem],
                device_id=(dp, h * NB + who), device_id_type=MESH,
            ).start()
            return 0

        lax.fori_loop(1, NB, go, 0)

    half_of = rab.at[0, pl.ds(0, NB), 0]
    pltpu.make_async_copy(half_of, half_of, z_r.at[0]).wait()
    stage_a(0)
    far(sa, yb, False)
    for b in range(NB):
        ps[b, :, :] = yb[CH * b : CH * b + CH, :].astype(BF16)

    def send_part(j, _):
        who = lax.rem(r + j, NB)
        at = jnp.where(h == 0, who, NB - 1 - who)
        pltpu.make_async_remote_copy(
            src_ref=ps.at[at], dst_ref=pt.at[r], send_sem=y_s.at[3], recv_sem=y_r.at[3],
            device_id=(dp, (1 - h) * NB + who), device_id_type=MESH,
        ).start()
        return 0

    lax.fori_loop(0, NB, send_part, 0)

    pltpu.make_async_copy(half_of, half_of, z_r.at[3]).wait()
    stage_b(0)
    near(g)
    pack_a(0)
    give(lambda at: ys.at[0, at, 0], yt.at[h * NB + r, 0], 0)
    keep[...] = yb[...]

    for j in range(1, 4):
        rows = pl.ds(pl.multiple_of(lax.rem(seat + 4 - j, 4) * 128, 128), 128)
        pltpu.make_async_copy(ho.at[rows], ho.at[rows], ex_r.at[j]).wait()

    def other(i, _):
        for u in range(U):
            c = i * U + u
            build_taps(ho, c * 32, 32, go.at[c])
        return 0

    lax.fori_loop(0, CH // U, other, 0)
    pltpu.make_async_copy(rab.at[1], rab.at[1], z_r.at[1]).wait()
    stage_a(1)
    stage_b(1)
    near(go)
    pack_a(1)
    pack_b(1, yb)
    give(lambda at: ys.at[1, at], yt.at[(1 - h) * NB + r], 2)

    pltpu.make_async_copy(rr, rr, z_r.at[2]).wait()
    for b in range(NB):
        sr[CH * b : CH * b + CH, :] = rr[b, :, :].astype(F32)
    far(sr, keep, True)
    pack_b(0, keep)
    give(lambda at: ys.at[0, at, 1], yt.at[h * NB + r, 1], 1)

    def turn_back(role, y):
        y = lax.dot_general(
            flips[role], y, (((1,), (1,)), ((), ())), preferred_element_type=F32
        ).astype(BF16)
        return jnp.dot(y, flips[role], preferred_element_type=F32)

    def source(role, i):
        return jnp.where(h == 1 - role, D // 128 - 1 - i, i)

    own_rows = yt.at[pl.ds(0, NB), 0]
    both_rows = yt.at[pl.ds(0, NB)]
    pltpu.make_async_copy(own_rows, own_rows, y_r.at[0]).wait()
    pltpu.make_async_copy(both_rows, both_rows, y_r.at[2]).wait()
    for i in range(8):
        y = yt[pl.ds(8 * source(0, i), 8), 0, :, :].reshape(128, POS)
        col = pl.ds(128 * i, 128)
        o[0, :, col] = o[0, :, col] * turn_back(0, y)
    def add_strand(i):
        y = yt[pl.ds(8 * source(1, i), 8), 1, :, :].reshape(128, POS)
        col = pl.ds(128 * i, 128)
        comb[:, col] = (o[0, :, col] + o[1, :, col] * turn_back(1, y)).astype(BF16)

    def project(rows, col):
        return jnp.dot(comb[:, rows], wv[rows, col], preferred_element_type=F32)

    pltpu.make_async_copy(weight, wv, in_sem.at[3]).wait()
    pltpu.make_async_copy(own_rows, own_rows, y_r.at[1]).wait()
    for i in range(4, 8):
        add_strand(i)
    for i in range(4):
        col = pl.ds(256 * i, 256)
        o[0, :, col] = project(pl.ds(D // 2, D // 2), col) if i >= 2 else o[0, :, col]
    pltpu.make_async_copy(pt, pt, y_r.at[3]).wait()
    mine = pl.ds((1 - h) * NB, NB)
    yt[mine, 1, :, :] = (yt[mine, 1, :, :].astype(F32) + pt[...].astype(F32)).astype(BF16)
    for i in range(4):
        add_strand(i)
    for i in range(4):
        col = pl.ds(256 * i, 256)
        if i >= 2:
            total = o[0, :, col] + project(pl.ds(0, D // 2), col)
        else:
            total = project(pl.ds(0, D), col)
        out[:, col] = total.astype(BF16)

    for k in range(2):
        left = yt.at[pl.ds(0, NB - 1), 0]
        pltpu.make_async_copy(left, left, z_s.at[3 * k]).wait()
        pltpu.make_async_copy(left, left, y_s.at[k]).wait()
    left = z.at[pl.ds(0, NB - 1)]
    pltpu.make_async_copy(left, left, z_s.at[1]).wait()
    left = z.at[pl.ds(0, NB), 0]
    pltpu.make_async_copy(left, left, z_s.at[2]).wait()
    left = yt.at[pl.ds(0, NB - 1)]
    pltpu.make_async_copy(left, left, y_s.at[2]).wait()
    pltpu.make_async_copy(ps, ps, y_s.at[3]).wait()
    cross.wait_send()
    for j in range(1, 4):
        mate_copy(j).wait_send()
    pltpu.make_async_copy(hsend.at[0], hsend.at[0], halo_s.at[0]).wait()

    @pl.when(slot > 0)
    def _():
        pltpu.make_async_copy(hsend.at[1], hsend.at[1], halo_s.at[1]).wait()


def per_device(fwd_proj, rev_proj, tokens, short_taps, long_kernel, skip_gain, out_weight):
    vmem = pltpu.VMEM
    dma = pltpu.SemaphoreType.DMA
    anywhere = pl.BlockSpec(memory_space=pl.ANY)
    local = pl.BlockSpec(memory_space=vmem)
    scratch = [
        vmem((2, POS, 3 * D), BF16),
        vmem((2, POS + 8, 3 * D), F32),
        vmem((2, 2 * TILES, 128), F32),
        vmem((2, 2 * TILES, 128), BF16),
        vmem((2, 2 * TILES, 128), BF16),
        vmem((2, 2 * TILES, 128), F32),
        vmem((D // CH, 2, CH, POS), BF16),
        vmem((CH * 64, 128), F32),
        vmem((CH * 64, 128), BF16),
        vmem((CH * 32, 128), BF16),
        vmem((CH * 32, 128), BF16),
        vmem((CH, 1024, 256), BF16),
        vmem((CH, 512, 256), BF16),
        vmem((2, NB, 2, CH, POS), BF16),
        vmem((NB, CH, POS), BF16),
        vmem((NB * CH, POS), F32),
        vmem((NB * CH, POS), F32),
        vmem((NB * CH, POS), F32),
        vmem((NB * CH, POS), F32),
        vmem((NB * CH, POS), F32),
        vmem((NB * CH, POS), F32),
        vmem((2, NB, 2, CH, POS), BF16),
        vmem((NB, CH, POS), BF16),
        vmem((D // CH, 2, CH, POS), BF16),
        vmem((NB, CH, POS), BF16),
        vmem((2, POS, D), F32),
        vmem((POS, D), BF16),
        vmem((D, D), BF16),
        vmem((CH, 8192), F32),
    ]
    scratch += [vmem((8 * NB, 512), BF16)] * W
    scratch += [vmem((4 * 48, 1024), BF16)] * W
    scratch += [vmem((2, 4, ROWS, 128), F32)] * W
    scratch += [vmem((2, 4, 8 + NB, 256), F32)] * W
    scratch += [vmem((4, 48, 256), F32)] * W
    scratch += [
        dma((4,)),
        dma((2,)), dma((2,)),
        dma((4,)), dma((4,)),
        dma((4,)), dma((4,)),
        dma((4,)), dma((4,)),
    ]
    return pl.pallas_call(
        kernel,
        out_shape=jax.ShapeDtypeStruct((POS, D), BF16),
        in_specs=[anywhere, anywhere, local, local, anywhere, local, anywhere],
        out_specs=local,
        scratch_shapes=scratch,
        name="hyena",
        compiler_params=pltpu.CompilerParams(
            collective_id=0, has_side_effects=True, vmem_limit_bytes=60 * 2**20
        ),
    )(
        fwd_proj, rev_proj, tokens.reshape(1, POS), short_taps, long_kernel,
        skip_gain.reshape(1, CH), out_weight,
    )


def solution(mesh):
    in_specs = (
        P(("dp", "ctx"), None),
        P(("dp", "ctx"), None),
        P(("dp", "ctx")),
        P(),
        P("ctx", None),
        P("ctx"),
        P(),
    )
    out_specs = P(("dp", "ctx"), None)
    return jax.shard_map(
        per_device, mesh=mesh, in_specs=in_specs, out_specs=out_specs, check_vma=False
    )
```
